512 devices in a mesh: tm: 16 (over x_lo, y, core), patch: 32 (over z, x_hi).
Axes of the slice: x: 4 (x_hi: 2, x_lo: 2; x = x_hi * 2 + x_lo), y: 4, z: 16, core: 2. Of those that a mesh axis runs over, the one named last changes fastest.
Arguments:
- query_vectors: bfloat16 [16, 16, 256, 2048], P(None, 'tm', 'patch'), may hold values from -32 to 32
- key_vectors: bfloat16 [16, 16, 256, 2048], P(None, 'tm', 'patch'), may hold values from -32 to 32
- value_vectors: bfloat16 [16, 16, 256, 2048], P(None, 'tm', 'patch'), may hold values from -6 to 6
- grad_output: bfloat16 [16, 16, 256, 2048], P(None, 'tm', 'patch'), may hold values from -6 to 6
- time_bias: float32 [16, 16], replicated, may hold values from -26 to 2
Outputs:
- grad_queries: bfloat16 [16, 16, 256, 2048], P(None, 'tm', 'patch')
- grad_keys: bfloat16 [16, 16, 256, 2048], P(None, 'tm', 'patch')
- grad_values: bfloat16 [16, 16, 256, 2048], P(None, 'tm', 'patch')
- grad_bias: float32 [16, 16], replicated
The draws below stay inside these ranges and needn't reach their ends.
All inputs are finite; a program needn't handle non-finite values.
Results may differ from the reference program's by a relative error of at most 0.0069.
Values may be sent and summed in bfloat16 or wider, within the bound.
A program may use at most 64 MiB of HBM per device.

```python
import math
import jax
import jax.numpy as jnp
from jax import lax

H = 16
HD = 128
CLIPS = 16
FRAMES = 16
PATCHES = 256


def shared_base(key):
    ground_key = jax.random.fold_in(key, 101)
    ground = jnp.clip(jax.random.normal(ground_key, (CLIPS, FRAMES, PATCHES, H * HD), jnp.float32), -5.0, 5.0)
    return ground


def draw_query_vectors(key, part):
    ground = shared_base(key)
    return ground.astype(jnp.bfloat16)


def draw_key_vectors(key, part):
    key = jax.random.fold_in(key, 5)
    fresh_draw = jnp.clip(jax.random.normal(key, (CLIPS, FRAMES, PATCHES, H * HD), jnp.float32), -5.0, 5.0)
    return fresh_draw.astype(jnp.bfloat16)


def draw_time_bias(key, part):
    key = jax.random.fold_in(key, 9)
    slope_key = jax.random.fold_in(key, 1)
    jitter_key = jax.random.fold_in(key, 2)
    unit = jax.random.uniform(slope_key, (H, 1), jnp.float32, 0.0, 1.0)
    slopes = jnp.exp(jnp.log(0.03) + unit * (jnp.log(1.5) - jnp.log(0.03)))
    jitter = jnp.clip(0.5 * jax.random.normal(jitter_key, (H, FRAMES), jnp.float32), -1.5, 1.5)
    offsets = jnp.arange(FRAMES, dtype=jnp.float32)[None, :]
    return -slopes * offsets + jitter


def level_of(stream_key, dims, cuts, least, high):
    gain, own = 1.0, jax.random.fold_in(stream_key, 6)
    for dim, blocks in cuts:
        steps = jnp.exp(jax.random.uniform(jax.random.fold_in(own, dim), (blocks,), jnp.float32, least / len(cuts), high / len(cuts)))
        gain = gain * jnp.repeat(steps, dims[dim] // blocks).reshape([-1 if axis == dim else 1 for axis in range(len(dims))])
    return gain


def normal_values(own_key, extent, spread, reach, shards=(), kind=jnp.bfloat16):
    drawn = spread * jax.random.normal(own_key, extent, jnp.float32)
    if shards:
        drawn = drawn * level_of(own_key, extent, shards, -0.22, 0.18)
    return jnp.clip(drawn, -reach, reach).astype(kind)


def setup_inputs(seed: int = 0) -> dict:
    streams_of = jax.random.split(jax.random.key(seed), 6)
    return {
        "query_vectors": draw_query_vectors(jax.random.fold_in(streams_of[5], 71), 0),
        "key_vectors": draw_key_vectors(jax.random.fold_in(streams_of[5], 71), 0),
        "value_vectors": normal_values(streams_of[2], (CLIPS, FRAMES, PATCHES, H * HD), 1.0, 6.0, ((1, 16), (2, 32))),
        "grad_output": normal_values(streams_of[3], (CLIPS, FRAMES, PATCHES, H * HD), 1.0, 6.0, ((1, 16), (2, 32))),
        "time_bias": draw_time_bias(jax.random.fold_in(streams_of[5], 71), 0),
    }


def score_table(bias_rows, frames):
    steps = jnp.arange(frames, dtype=jnp.int32)
    offsets = steps[:, None] - steps[None, :]
    onehot = (offsets[:, :, None] == steps[None, None, :]).astype(jnp.float32)
    table = jnp.einsum('hd,tud->htu', bias_rows, onehot, precision=lax.Precision.HIGHEST)
    return (table, offsets >= 0, onehot)

def attend_ref(query_heads, key_heads, value_heads, grad_heads, bias_rows):
    frames = query_heads.shape[1]
    score_scale = 1.0 / math.sqrt(query_heads.shape[4])
    table, causal, onehot = score_table(bias_rows, frames)
    query_wide = query_heads.astype(jnp.float32)
    key_wide = key_heads.astype(jnp.float32)
    value_wide = value_heads.astype(jnp.float32)
    grad_wide = grad_heads.astype(jnp.float32)
    highest = lax.Precision.HIGHEST
    scores = jnp.einsum('atxhd,auxhd->axhtu', query_wide, key_wide, precision=highest) * score_scale + table[None, None]
    scores = jnp.where(causal, scores, -jnp.inf)
    row_max = lax.optimization_barrier(jnp.max(scores, axis=-1, keepdims=True))
    expon = jnp.exp(scores - row_max)
    weights = expon / lax.optimization_barrier(jnp.sum(expon, axis=-1, keepdims=True))
    weights_wide = lax.optimization_barrier(weights.astype(jnp.bfloat16)).astype(jnp.float32)
    attended = jnp.einsum('axhtu,auxhd->atxhd', weights_wide, value_wide, precision=highest)
    rowdot = jnp.einsum('atxhd,atxhd->axht', grad_wide, attended, precision=highest)
    grad_weights = jnp.einsum('atxhd,auxhd->axhtu', grad_wide, value_wide, precision=highest)
    grad_scores = weights * (grad_weights - rowdot[..., None])
    bias_terms = jnp.einsum('axhtu,tud->axhd', grad_scores, onehot, precision=highest)
    grad_low = lax.optimization_barrier(grad_scores.astype(jnp.bfloat16)).astype(jnp.float32)
    grad_query = (jnp.einsum('axhtu,auxhd->atxhd', grad_low, key_wide, precision=highest) * score_scale).astype(jnp.bfloat16)
    grad_key = (jnp.einsum('axhtu,atxhd->auxhd', grad_low, query_wide, precision=highest) * score_scale).astype(jnp.bfloat16)
    grad_value = jnp.einsum('axhtu,atxhd->auxhd', weights_wide, grad_wide, precision=highest).astype(jnp.bfloat16)
    return (grad_query, grad_key, grad_value, bias_terms)

def reference(query_vectors, key_vectors, value_vectors, grad_output, time_bias):
    head_count = time_bias.shape[0]
    head_dim = query_vectors.shape[3] // head_count
    flat_shape = query_vectors.shape[1:]

    def per_clip(clip_block):
        split_heads = [item.reshape((1, item.shape[0], item.shape[1], head_count, head_dim)) for item in clip_block]
        grad_query, grad_key, grad_value, bias_terms = attend_ref(split_heads[0], split_heads[1], split_heads[2], split_heads[3], time_bias)
        return (grad_query.reshape(flat_shape), grad_key.reshape(flat_shape), grad_value.reshape(flat_shape), lax.optimization_barrier(jnp.sum(bias_terms, axis=(0, 1))))
    grad_query, grad_key, grad_value, bias_terms = lax.map(per_clip, (query_vectors, key_vectors, value_vectors, grad_output))
    return (grad_query, grad_key, grad_value, lax.optimization_barrier(jnp.sum(bias_terms, axis=0)))
```

```python
import functools
import math

import jax
import jax.numpy as jnp
from jax import lax
from jax.experimental import pallas as pl
from jax.experimental.pallas import tpu as pltpu
from jax.sharding import PartitionSpec as P

MESH = pl.DeviceIdType.MESH
GROUP = 16
NEG = -1e30


def body(frames, span, parts, q_hbm, k_hbm, v_hbm, g_hbm, bias_ref, oq_hbm, ok_hbm, ov_hbm, ob_ref,
         held, back, table, acc, mine, shares, rows_all,
         in_sem, in_sent, out_sem, out_sent, share_sem, share_sent, row_sem, row_sent):
    me = lax.axis_index("tm")
    place = lax.axis_index("patch")
    rows, dim = held.shape[2], held.shape[3]
    step_rows = rows // parts
    inputs = (q_hbm, k_hbm, v_hbm, g_hbm)
    outputs = (oq_hbm, ok_hbm, ov_hbm)
    scale = 1.0 / math.sqrt(dim)

    def head_columns(head):
        return pl.ds(pl.multiple_of(head * dim, dim), dim)

    barrier = pltpu.get_barrier_semaphore()
    for off in range(1, frames):
        pl.semaphore_signal(barrier, inc=1, device_id={"tm": lax.rem(me + off, frames)}, device_id_type=MESH)
    for off in range(1, span):
        pl.semaphore_signal(barrier, inc=1, device_id={"patch": lax.rem(place + off, span)}, device_id_type=MESH)
    pl.semaphore_wait(barrier, frames - 1 + span - 1)

    def send_part(part, carry):
        part_rows = pl.ds(pl.multiple_of(part * step_rows, step_rows), step_rows)
        for a in range(4):
            pltpu.make_async_copy(
                inputs[a].at[part_rows, head_columns(me)], held.at[a, me, part_rows], in_sem.at[part]).start()
        for off in range(1, frames):
            head = lax.rem(me + off, frames)
            for a in range(4):
                pltpu.make_async_remote_copy(
                    src_ref=inputs[a].at[part_rows, head_columns(head)],
                    dst_ref=held.at[a, me, part_rows],
                    send_sem=in_sent, recv_sem=in_sem.at[part],
                    device_id={"tm": head}, device_id_type=MESH).start()
        return carry

    lax.fori_loop(0, parts, send_part, 0)

    size = frames * GROUP
    u_row = lax.broadcasted_iota(jnp.int32, (size, size), 0)
    t_col = lax.broadcasted_iota(jnp.int32, (size, size), 1)
    same = (u_row % GROUP) == (t_col % GROUP)
    offset = jnp.where(same, t_col // GROUP - u_row // GROUP, -1)
    filled = jnp.full((size, size), NEG, jnp.float32)
    for d in range(frames):
        filled = jnp.where(offset == d, bias_ref[me, d], filled)
    table[...] = filled
    acc[...] = jnp.zeros_like(acc)

    contract_last = (((1,), (1,)), ((), ()))
    contract_first = (((0,), (0,)), ((), ()))

    def attend(block):
        take = pl.ds(pl.multiple_of(block * GROUP, GROUP), GROUP)
        q, k, v, g = (held[a, :, take, :].reshape(size, dim) for a in range(4))
        scores = lax.dot_general(k, q, contract_last, preferred_element_type=jnp.float32) * scale + table[...]
        expon = jnp.exp(scores - jnp.max(scores, axis=0, keepdims=True))
        weights = expon * (1.0 / jnp.sum(expon, axis=0, keepdims=True))
        low = weights.astype(jnp.bfloat16)
        grad_weights = lax.dot_general(v, g, contract_last, preferred_element_type=jnp.float32)
        rowdot = jnp.sum(low.astype(jnp.float32) * grad_weights, axis=0, keepdims=True)
        grad_scores = weights * (grad_weights - rowdot)
        acc[...] += grad_scores
        grad_low = grad_scores.astype(jnp.bfloat16)
        dv = jnp.dot(low, g, preferred_element_type=jnp.float32)
        dk = jnp.dot(grad_low, q, preferred_element_type=jnp.float32) * scale
        dq = lax.dot_general(grad_low, k, contract_first, preferred_element_type=jnp.float32) * scale
        for a, grad in enumerate((dq, dk, dv)):
            back[a, :, take, :] = grad.astype(jnp.bfloat16).reshape(frames, GROUP, dim)

    def work_part(part, carry):
        part_rows = pl.ds(pl.multiple_of(part * step_rows, step_rows), step_rows)
        here = held.at[:, :, part_rows]
        pltpu.make_async_copy(here, here, in_sem.at[part]).wait()
        for i in range(step_rows // GROUP):
            attend(part * (step_rows // GROUP) + i)
        for off in range(1, frames):
            frame = lax.rem(me + off, frames)
            for a in range(3):
                pltpu.make_async_remote_copy(
                    src_ref=back.at[a, frame, part_rows],
                    dst_ref=outputs[a].at[part_rows, head_columns(me)],
                    send_sem=out_sent, recv_sem=out_sem.at[a],
                    device_id={"tm": frame}, device_id_type=MESH).start()
        for a in range(3):
            pltpu.make_async_copy(
                back.at[a, me, part_rows], outputs[a].at[part_rows, head_columns(me)], out_sem.at[a]).start()
        return carry

    lax.fori_loop(0, parts, work_part, 0)

    by_frame = jnp.sum(acc[...].reshape(frames, GROUP, size), axis=1)
    u_small = lax.broadcasted_iota(jnp.int32, (frames, size), 0)
    t_small = lax.broadcasted_iota(jnp.int32, (frames, size), 1) // GROUP
    lane = lax.broadcasted_iota(jnp.int32, (1, 128), 1)
    row = jnp.zeros((1, 128), jnp.float32)
    for d in range(frames):
        total = jnp.sum(jnp.where(t_small - u_small == d, by_frame, 0.0))
        row = jnp.where(lane == d, total, row)
    mine[...] = jnp.broadcast_to(row, mine.shape)
    own = pltpu.make_async_copy(mine, shares.at[place], share_sem)
    own.start()
    for off in range(1, span):
        pltpu.make_async_remote_copy(
            src_ref=mine, dst_ref=shares.at[place], send_sem=share_sent, recv_sem=share_sem,
            device_id={"patch": lax.rem(place + off, span)}, device_id_type=MESH).start()
    pltpu.make_async_copy(shares, shares, share_sem).wait()
    sent = shares.at[pl.ds(0, span - 1)]
    pltpu.make_async_copy(sent, sent, share_sent).wait()
    mine[...] = jnp.sum(shares[...], axis=0)
    own = pltpu.make_async_copy(mine, rows_all.at[me], row_sem)
    own.start()
    for off in range(1, frames):
        pltpu.make_async_remote_copy(
            src_ref=mine, dst_ref=rows_all.at[me], send_sem=row_sent, recv_sem=row_sem,
            device_id={"tm": lax.rem(me + off, frames)}, device_id_type=MESH).start()
    pltpu.make_async_copy(rows_all, rows_all, row_sem).wait()
    sent = rows_all.at[pl.ds(0, frames - 1)]
    pltpu.make_async_copy(sent, sent, row_sent).wait()
    for h in range(frames):
        ob_ref[pl.ds(h, 1), :] = rows_all[h, 0:1, 0:frames]

    sent = held.at[:, pl.ds(0, frames - 1)]
    pltpu.make_async_copy(sent, sent, in_sent).wait()
    sent = back.at[:, pl.ds(0, frames - 1)]
    pltpu.make_async_copy(sent, sent, out_sent).wait()
    for a in range(3):
        pltpu.make_async_copy(outputs[a], outputs[a], out_sem.at[a]).wait()


def per_device(span, query, key, value, grad, time_bias):
    clips, _, patches, width = query.shape
    heads, frames = time_bias.shape
    dim = width // heads
    rows = clips * patches
    flat = [item.reshape(rows, width) for item in (query, key, value, grad)]
    parts = 4
    any_space = pl.BlockSpec(memory_space=pl.ANY)
    size = frames * GROUP
    dma = pltpu.SemaphoreType.DMA
    out = pl.pallas_call(
        functools.partial(body, frames, span, parts),
        out_shape=[jax.ShapeDtypeStruct((rows, width), jnp.bfloat16)] * 3
        + [jax.ShapeDtypeStruct((heads, frames), jnp.float32)],
        in_specs=[any_space] * 4 + [pl.BlockSpec(memory_space=pltpu.SMEM)],
        out_specs=[any_space] * 3 + [pl.BlockSpec(memory_space=pltpu.VMEM)],
        scratch_shapes=[
            pltpu.VMEM((4, frames, rows, dim), jnp.bfloat16),
            pltpu.VMEM((3, frames, rows, dim), jnp.bfloat16),
            pltpu.VMEM((size, size), jnp.float32),
            pltpu.VMEM((size, size), jnp.float32),
            pltpu.VMEM((8, 128), jnp.float32),
            pltpu.VMEM((span, 8, 128), jnp.float32),
            pltpu.VMEM((frames, 8, 128), jnp.float32),
            dma((parts,)), dma, dma((3,)), dma, dma, dma, dma, dma,
        ],
        compiler_params=pltpu.CompilerParams(
            collective_id=0, has_side_effects=True, vmem_limit_bytes=40 * 2**20),
    )(*flat, time_bias)
    return tuple(item.reshape(query.shape) for item in out[:3]) + (out[3],)


def solution(mesh):
    placed = P(None, "tm", "patch", None)
    return jax.shard_map(
        functools.partial(per_device, mesh.shape["patch"]),
        mesh=mesh,
        in_specs=(placed, placed, placed, placed, P()),
        out_specs=(placed, placed, placed, P()),
        check_vma=False,
    )
```

```python
import functools
import math

import jax
import jax.numpy as jnp
from jax import lax
from jax.experimental import pallas as pl
from jax.experimental.pallas import tpu as pltpu
from jax.sharding import PartitionSpec as P

MESH = pl.DeviceIdType.MESH
GROUP = 16
NEG = -1e30
FIRST, SHARER = 0, 1


def body(frames, span, parts, lag, q_hbm, k_hbm, v_hbm, g_hbm, bias_hbm, oq_hbm, ok_hbm, ov_hbm, ob_ref,
         bias_ref, held, back, table, acc, mine, gathered, group, shares, result,
         in_sem, in_sent, out_sem, out_sent, gather_sem, gather_sent, share_sem, share_sent, result_sem, result_sent,
         bias_sem, go_sem):
    me = lax.axis_index("tm")
    place = lax.axis_index("patch")
    rows, dim = held.shape[2], held.shape[3]
    step_rows = rows // parts
    inputs = (q_hbm, k_hbm, v_hbm, g_hbm)
    outputs = (oq_hbm, ok_hbm, ov_hbm)
    scale = 1.0 / math.sqrt(dim)

    def head_columns(head):
        return pl.ds(pl.multiple_of(head * dim, dim), dim)

    bias_copy = pltpu.make_async_copy(bias_hbm, bias_ref, bias_sem)
    bias_copy.start()

    barrier = pltpu.get_barrier_semaphore()
    for off in range(1, frames):
        peer = lax.rem(me + off, frames)

        @pl.when(peer != SHARER)
        def _():
            pl.semaphore_signal(barrier, inc=1, device_id={"tm": peer}, device_id_type=MESH)

    @pl.when(me == SHARER)
    def _():
        for off in range(1, span):
            pl.semaphore_signal(barrier, inc=1, device_id={"patch": lax.rem(place + off, span)}, device_id_type=MESH)

    @pl.when(me != SHARER)
    def _():
        pl.semaphore_wait(barrier, frames - 1)

    @pl.when(me == FIRST)
    def _():
        pl.semaphore_signal(go_sem, inc=1, device_id={"tm": SHARER}, device_id_type=MESH)

    @pl.when(me == SHARER)
    def _():
        pl.semaphore_wait(go_sem, 1)

    def send_part(part, carry):
        part_rows = pl.ds(pl.multiple_of(part * step_rows, step_rows), step_rows)
        for a in range(4):
            pltpu.make_async_copy(
                inputs[a].at[part_rows, head_columns(me)], held.at[a, me, part_rows], in_sem.at[part]).start()
        for off in range(1, frames):
            head = lax.rem(me + off, frames)
            for a in range(4):
                pltpu.make_async_remote_copy(
                    src_ref=inputs[a].at[part_rows, head_columns(head)],
                    dst_ref=held.at[a, me, part_rows],
                    send_sem=in_sent, recv_sem=in_sem.at[part],
                    device_id={"tm": head}, device_id_type=MESH).start()
        return carry

    lax.fori_loop(0, parts, send_part, 0)

    size = frames * GROUP
    u_row = lax.broadcasted_iota(jnp.int32, (size, size), 0)
    t_col = lax.broadcasted_iota(jnp.int32, (size, size), 1)
    same = (u_row % GROUP) == (t_col % GROUP)
    offset = jnp.where(same, t_col // GROUP - u_row // GROUP, -1)
    bias_copy.wait()
    filled = jnp.full((size, size), NEG, jnp.float32)
    for d in range(frames):
        filled = jnp.where(offset == d, bias_ref[me, d], filled)
    table[...] = filled
    acc[...] = jnp.zeros_like(acc)

    contract_last = (((1,), (1,)), ((), ()))
    contract_first = (((0,), (0,)), ((), ()))

    def attend(block):
        take = pl.ds(pl.multiple_of(block * GROUP, GROUP), GROUP)
        q, k, v, g = (held[a, :, take, :].reshape(size, dim) for a in range(4))
        scores = lax.dot_general(k, q, contract_last, preferred_element_type=jnp.float32) * scale + table[...]
        expon = jnp.exp(scores - jnp.max(scores, axis=0, keepdims=True))
        weights = expon * (1.0 / jnp.sum(expon, axis=0, keepdims=True))
        low = weights.astype(jnp.bfloat16)
        grad_weights = lax.dot_general(v, g, contract_last, preferred_element_type=jnp.float32)
        rowdot = jnp.sum(low.astype(jnp.float32) * grad_weights, axis=0, keepdims=True)
        grad_scores = weights * (grad_weights - rowdot)
        acc[...] += grad_scores
        grad_low = grad_scores.astype(jnp.bfloat16)
        dv = jnp.dot(low, g, preferred_element_type=jnp.float32)
        dk = jnp.dot(grad_low, q, preferred_element_type=jnp.float32) * scale
        dq = lax.dot_general(grad_low, k, contract_first, preferred_element_type=jnp.float32) * scale
        for a, grad in enumerate((dq, dk, dv)):
            back[a, :, take, :] = grad.astype(jnp.bfloat16).reshape(frames, GROUP, dim)

    def send_back(part, carry):
        part_rows = pl.ds(pl.multiple_of(part * step_rows, step_rows), step_rows)
        for off in range(1, frames):
            frame = lax.rem(me + off, frames)
            for a in range(3):
                pltpu.make_async_remote_copy(
                    src_ref=back.at[a, frame, part_rows],
                    dst_ref=outputs[a].at[part_rows, head_columns(me)],
                    send_sem=out_sent, recv_sem=out_sem.at[a],
                    device_id={"tm": frame}, device_id_type=MESH).start()
        for a in range(3):
            pltpu.make_async_copy(
                back.at[a, me, part_rows], outputs[a].at[part_rows, head_columns(me)], out_sem.at[a]).start()
        return carry

    def work_part(part, carry):
        here = held.at[:, :, pl.ds(pl.multiple_of(part * step_rows, step_rows), step_rows)]
        pltpu.make_async_copy(here, here, in_sem.at[part]).wait()
        for i in range(step_rows // GROUP):
            attend(part * (step_rows // GROUP) + i)

        @pl.when(part >= lag)
        def _():
            send_back(part - lag, 0)

        return carry

    lax.fori_loop(0, parts, work_part, 0)

    by_frame = jnp.sum(acc[...].reshape(frames, GROUP, size), axis=1)
    u_small = lax.broadcasted_iota(jnp.int32, (frames, size), 0)
    t_small = lax.broadcasted_iota(jnp.int32, (frames, size), 1) // GROUP
    sums = [jnp.sum(jnp.where(t_small - u_small == d, by_frame, 0.0), axis=0, keepdims=True) for d in range(frames)]
    column = jnp.sum(jnp.concatenate(sums, axis=0), axis=1, keepdims=True)
    lane = lax.broadcasted_iota(jnp.int32, mine.shape, 1)
    mine[...] = jnp.where(lane == me, column, 0.0)

    @pl.when(me != SHARER)
    def _():
        pltpu.make_async_remote_copy(
            src_ref=mine, dst_ref=gathered.at[me], send_sem=gather_sent, recv_sem=gather_sem,
            device_id={"tm": SHARER}, device_id_type=MESH).start()

    lax.fori_loop(parts - lag, parts, send_back, 0)

    @pl.when(me == SHARER)
    def _():
        pltpu.make_async_copy(mine, gathered.at[me], gather_sem).start()
        pltpu.make_async_copy(gathered, gathered, gather_sem).wait()
        group[...] = jnp.sum(gathered[...], axis=0)
        pl.semaphore_wait(barrier, span - 1)
        pltpu.make_async_copy(group, shares.at[place], share_sem).start()
        for off in range(1, span):
            pltpu.make_async_remote_copy(
                src_ref=group, dst_ref=shares.at[place], send_sem=share_sent, recv_sem=share_sem,
                device_id={"patch": lax.rem(place + off, span)}, device_id_type=MESH).start()
        pltpu.make_async_copy(shares, shares, share_sem).wait()
        result[...] = jnp.sum(shares[...], axis=0)
        for off in range(1, frames):
            pltpu.make_async_remote_copy(
                src_ref=result, dst_ref=result, send_sem=result_sent, recv_sem=result_sem,
                device_id={"tm": lax.rem(me + off, frames)}, device_id_type=MESH).start()
        sent = shares.at[pl.ds(0, span - 1)]
        pltpu.make_async_copy(sent, sent, share_sent).wait()
        sent = gathered.at[pl.ds(0, frames - 1)]
        pltpu.make_async_copy(sent, sent, result_sent).wait()

    @pl.when(me != SHARER)
    def _():
        pltpu.make_async_copy(mine, mine, gather_sent).wait()
        pltpu.make_async_copy(result, result, result_sem).wait()

    ob_ref[...] = result[...]

    sent = held.at[:, pl.ds(0, frames - 1)]
    pltpu.make_async_copy(sent, sent, in_sent).wait()
    sent = back.at[:, pl.ds(0, frames - 1)]
    pltpu.make_async_copy(sent, sent, out_sent).wait()
    for a in range(3):
        pltpu.make_async_copy(outputs[a], outputs[a], out_sem.at[a]).wait()


def finish(*refs):
    sources, targets, sem = refs[:3], refs[3:6], refs[6]
    copies = [pltpu.make_async_copy(a, b, sem.at[i]) for i, (a, b) in enumerate(zip(sources, targets))]
    for copy in copies:
        copy.start()
    for copy in copies:
        copy.wait()


def per_device(span, query, key, value, grad, time_bias):
    clips, _, patches, width = query.shape
    heads, frames = time_bias.shape
    dim = width // heads
    rows = clips * patches
    given = [item.reshape(rows, width) for item in (query, key, value, grad)] + [time_bias]
    given = [pltpu.with_memory_space_constraint(item, pltpu.HBM) for item in given]
    parts, lag = 8, 8
    any_space = pl.BlockSpec(memory_space=pl.ANY)
    size = frames * GROUP
    tile = (frames, 128)
    dma = pltpu.SemaphoreType.DMA
    out = pl.pallas_call(
        functools.partial(body, frames, span, parts, lag),
        out_shape=[jax.ShapeDtypeStruct((rows, width), jnp.bfloat16)] * 3
        + [jax.ShapeDtypeStruct(tile, jnp.float32)],
        in_specs=[any_space] * 5,
        out_specs=[any_space] * 3 + [pl.BlockSpec(memory_space=pltpu.VMEM)],
        scratch_shapes=[
            pltpu.SMEM((heads, frames), jnp.float32),
            pltpu.VMEM((4, frames, rows, dim), jnp.bfloat16),
            pltpu.VMEM((3, frames, rows, dim), jnp.bfloat16),
            pltpu.VMEM((size, size), jnp.float32),
            pltpu.VMEM((size, size), jnp.float32),
            pltpu.VMEM(tile, jnp.float32),
            pltpu.VMEM((frames,) + tile, jnp.float32),
            pltpu.VMEM(tile, jnp.float32),
            pltpu.VMEM((span,) + tile, jnp.float32),
            pltpu.VMEM(tile, jnp.float32),
            dma((parts,)), dma, dma((3,)), dma, dma, dma, dma, dma, dma, dma, dma,
            pltpu.SemaphoreType.REGULAR,
        ],
        compiler_params=pltpu.CompilerParams(
            collective_id=0, has_side_effects=True, vmem_limit_bytes=40 * 2**20),
    )(*given)
    grads = [pltpu.with_memory_space_constraint(item, pltpu.VMEM) for item in out[:3]]
    grads = pl.pallas_call(
        finish,
        out_shape=[jax.ShapeDtypeStruct((rows, width), jnp.bfloat16)] * 3,
        in_specs=[any_space] * 3,
        out_specs=[any_space] * 3,
        scratch_shapes=[dma((3,))],
        compiler_params=pltpu.CompilerParams(vmem_limit_bytes=2**20),
    )(*grads)
    return tuple(item.reshape(query.shape) for item in grads) + (out[3][:, :heads].T,)


def solution(mesh):
    placed = P(None, "tm", "patch", None)
    return jax.shard_map(
        functools.partial(per_device, mesh.shape["patch"]),
        mesh=mesh,
        in_specs=(placed, placed, placed, placed, P()),
        out_specs=(placed, placed, placed, P()),
        check_vma=False,
    )
```

```python
import functools
import math

import jax
import jax.numpy as jnp
from jax import lax
from jax.experimental import pallas as pl
from jax.experimental.pallas import tpu as pltpu
from jax.sharding import PartitionSpec as P

MESH = pl.DeviceIdType.MESH
GROUP = 16
NEG = -1e30
FIRST, SHARER = 0, 1


def body(frames, span, parts, early, late, q_hbm, k_hbm, v_hbm, g_hbm, bias_hbm, oq_hbm, ok_hbm, ov_hbm, ob_ref,
         bias_ref, held, back, table, acc, lows, mine, shares, total, result,
         in_sem, in_sent, out_sem, out_sent, share_sem, share_sent, result_sem, result_sent,
         bias_sem, go_sem, world_sem):
    me = lax.axis_index("tm")
    place = lax.axis_index("patch")
    rows, dim = held.shape[2], held.shape[3]
    inputs = (q_hbm, k_hbm, v_hbm, g_hbm)
    outputs = (oq_hbm, ok_hbm, ov_hbm)
    scale = 1.0 / math.sqrt(dim)

    def rows_of(block):
        return pl.ds(pl.multiple_of(block * GROUP, GROUP), GROUP)

    def head_columns(head):
        return pl.ds(pl.multiple_of(head * dim, dim), dim)

    bias_copy = pltpu.make_async_copy(bias_hbm, bias_ref, bias_sem)
    bias_copy.start()

    barrier = pltpu.get_barrier_semaphore()
    for off in range(1, frames):
        peer = lax.rem(me + off, frames)

        @pl.when(peer != SHARER)
        def _():
            pl.semaphore_signal(barrier, inc=1, device_id={"tm": peer}, device_id_type=MESH)

    @pl.when(me != SHARER)
    def _():
        pl.semaphore_wait(barrier, frames - 1)

    @pl.when(me == FIRST)
    def _():
        pl.semaphore_signal(go_sem, inc=1, device_id={"tm": SHARER}, device_id_type=MESH)

    @pl.when(me == SHARER)
    def _():
        pl.semaphore_wait(go_sem, 1)
        for off in range(1, span):
            pl.semaphore_signal(barrier, inc=1, device_id={"patch": lax.rem(place + off, span)}, device_id_type=MESH)

    def send_part(part, carry):
        part_rows = rows_of(part)
        for a in range(4):
            pltpu.make_async_copy(
                inputs[a].at[part_rows, head_columns(me)], held.at[a, me, part_rows], in_sem.at[part]).start()
        for off in range(1, frames):
            head = lax.rem(me + off, frames)
            for a in range(4):
                pltpu.make_async_remote_copy(
                    src_ref=inputs[a].at[part_rows, head_columns(head)],
                    dst_ref=held.at[a, me, part_rows],
                    send_sem=in_sent, recv_sem=in_sem.at[part],
                    device_id={"tm": head}, device_id_type=MESH).start()
        return carry

    lax.fori_loop(0, parts, send_part, 0)

    size = frames * GROUP
    u_row = lax.broadcasted_iota(jnp.int32, (size, size), 0)
    t_col = lax.broadcasted_iota(jnp.int32, (size, size), 1)
    same = (u_row % GROUP) == (t_col % GROUP)
    offset = jnp.where(same, t_col // GROUP - u_row // GROUP, -1)
    bias_copy.wait()
    filled = jnp.full((size, size), NEG, jnp.float32)
    for d in range(frames):
        filled = jnp.where(offset == d, bias_ref[me, d], filled)
    table[...] = filled
    acc[...] = jnp.zeros_like(acc)

    contract_last = (((1,), (1,)), ((), ()))
    contract_first = (((0,), (0,)), ((), ()))

    def block_of(a, block):
        return held[a, :, rows_of(block), :].reshape(size, dim)

    def weigh(block):
        q, k, v, g = (block_of(a, block) for a in range(4))
        scores = lax.dot_general(k, q, contract_last, preferred_element_type=jnp.float32) * scale + table[...]
        expon = jnp.exp(scores - jnp.max(scores, axis=0, keepdims=True))
        weights = expon * (1.0 / jnp.sum(expon, axis=0, keepdims=True))
        low = weights.astype(jnp.bfloat16)
        grad_weights = lax.dot_general(v, g, contract_last, preferred_element_type=jnp.float32)
        rowdot = jnp.sum(low.astype(jnp.float32) * grad_weights, axis=0, keepdims=True)
        grad_scores = weights * (grad_weights - rowdot)
        acc[...] += grad_scores
        return low, grad_scores.astype(jnp.bfloat16)

    def gradients(block, low, grad_low):
        q, k, g = (block_of(a, block) for a in (0, 1, 3))
        dv = jnp.dot(low, g, preferred_element_type=jnp.float32)
        dk = jnp.dot(grad_low, q, preferred_element_type=jnp.float32) * scale
        dq = lax.dot_general(grad_low, k, contract_first, preferred_element_type=jnp.float32) * scale
        for a, grad in enumerate((dq, dk, dv)):
            back[a, :, rows_of(block), :] = grad.astype(jnp.bfloat16).reshape(frames, GROUP, dim)

    def send_back(part, carry):
        part_rows = rows_of(part)
        for off in range(1, frames):
            frame = lax.rem(me + off, frames)
            for a in range(3):
                pltpu.make_async_remote_copy(
                    src_ref=back.at[a, frame, part_rows],
                    dst_ref=outputs[a].at[part_rows, head_columns(me)],
                    send_sem=out_sent, recv_sem=out_sem.at[a],
                    device_id={"tm": frame}, device_id_type=MESH).start()
        for a in range(3):
            pltpu.make_async_copy(
                back.at[a, me, part_rows], outputs[a].at[part_rows, head_columns(me)], out_sem.at[a]).start()
        return carry

    def await_part(part):
        here = held.at[:, :, rows_of(part)]
        pltpu.make_async_copy(here, here, in_sem.at[part]).wait()

    def work_part(part, carry):
        await_part(part)
        gradients(part, *weigh(part))

        @pl.when(jnp.logical_and(part == parts - 2, me == SHARER))
        def _():
            pl.semaphore_wait(barrier, span - 1)
            for off in range(1, frames):
                pl.semaphore_signal(
                    world_sem, inc=1, device_id={"tm": lax.rem(me + off, frames)}, device_id_type=MESH)

        return carry

    last = parts - 1
    lax.fori_loop(0, last, work_part, 0)
    lax.fori_loop(0, early, send_back, 0)
    await_part(last)
    low, grad_low = weigh(last)
    lows[0] = low
    lows[1] = grad_low

    by_frame = jnp.sum(acc[...].reshape(frames, GROUP, size), axis=1)
    u_small = lax.broadcasted_iota(jnp.int32, (frames, size), 0)
    t_small = lax.broadcasted_iota(jnp.int32, (frames, size), 1) // GROUP
    sums = [jnp.sum(jnp.where(t_small - u_small == d, by_frame, 0.0), axis=0, keepdims=True) for d in range(frames)]
    sums += [jnp.zeros((128 - frames, size), jnp.float32)]
    mine[...] = lax.dot_general(
        jnp.ones((8, size), jnp.float32), jnp.concatenate(sums, axis=0), contract_last,
        precision=lax.Precision.HIGHEST, preferred_element_type=jnp.float32)[0:1]

    @pl.when(me != SHARER)
    def _():
        pl.semaphore_wait(world_sem, 1)

    pltpu.make_async_copy(mine, shares.at[place], share_sem).start()
    for off in sorted(range(1, span), key=lambda off: -min(off, span - off)):
        pltpu.make_async_remote_copy(
            src_ref=mine, dst_ref=shares.at[place], send_sem=share_sent, recv_sem=share_sem,
            device_id={"patch": lax.rem(place + off, span)}, device_id_type=MESH).start()
    lax.fori_loop(early, early + 1, send_back, 0)
    gradients(last, lows[0], lows[1])
    lax.fori_loop(early + 1, parts - late, send_back, 0)
    pltpu.make_async_copy(shares, shares, share_sem).wait()
    total[...] = jnp.sum(shares[...], axis=0)
    pltpu.make_async_copy(total, result.at[me], result_sem).start()
    for off in range(1, frames):
        pltpu.make_async_remote_copy(
            src_ref=total, dst_ref=result.at[me], send_sem=result_sent, recv_sem=result_sem,
            device_id={"tm": lax.rem(me + off, frames)}, device_id_type=MESH).start()
    lax.fori_loop(parts - late, parts, send_back, 0)
    pltpu.make_async_copy(result, result, result_sem).wait()
    for h in range(frames):
        ob_ref[pl.ds(h, 1), :] = result[h][:, 0:frames]
    sent = shares.at[pl.ds(0, span - 1)]
    pltpu.make_async_copy(sent, sent, share_sent).wait()
    sent = result.at[pl.ds(0, frames - 1)]
    pltpu.make_async_copy(sent, sent, result_sent).wait()

    sent = held.at[:, pl.ds(0, frames - 1)]
    pltpu.make_async_copy(sent, sent, in_sent).wait()
    sent = back.at[:, pl.ds(0, frames - 1)]
    pltpu.make_async_copy(sent, sent, out_sent).wait()
    for a in range(3):
        pltpu.make_async_copy(outputs[a], outputs[a], out_sem.at[a]).wait()


def finish(*refs):
    sources, targets, sem = refs[:4], refs[4:8], refs[8]
    copies = [pltpu.make_async_copy(a, b, sem.at[i]) for i, (a, b) in enumerate(zip(sources, targets))]
    for copy in copies:
        copy.start()
    for copy in copies:
        copy.wait()


def per_device(span, query, key, value, grad, time_bias):
    clips, _, patches, width = query.shape
    heads, frames = time_bias.shape
    dim = width // heads
    rows = clips * patches
    given = [item.reshape(rows, width) for item in (query, key, value, grad)] + [time_bias]
    given = [pltpu.with_memory_space_constraint(item, pltpu.HBM) for item in given]
    parts, early, late = rows // GROUP, 1, 1
    any_space = pl.BlockSpec(memory_space=pl.ANY)
    size = frames * GROUP
    dma = pltpu.SemaphoreType.DMA
    out = pl.pallas_call(
        functools.partial(body, frames, span, parts, early, late),
        out_shape=[jax.ShapeDtypeStruct((rows, width), jnp.bfloat16)] * 3
        + [jax.ShapeDtypeStruct((heads, frames), jnp.float32)],
        in_specs=[any_space] * 5,
        out_specs=[any_space] * 3 + [pl.BlockSpec(memory_space=pltpu.VMEM)],
        scratch_shapes=[
            pltpu.SMEM((heads, frames), jnp.float32),
            pltpu.VMEM((4, frames, rows, dim), jnp.bfloat16),
            pltpu.VMEM((3, frames, rows, dim), jnp.bfloat16),
            pltpu.VMEM((size, size), jnp.float32),
            pltpu.VMEM((size, size), jnp.float32),
            pltpu.VMEM((2, size, size), jnp.bfloat16),
            pltpu.VMEM((1, 128), jnp.float32),
            pltpu.VMEM((span, 1, 128), jnp.float32),
            pltpu.VMEM((1, 128), jnp.float32),
            pltpu.VMEM((frames, 1, 128), jnp.float32),
            dma((parts,)), dma, dma((3,)), dma, dma, dma, dma, dma, dma,
            pltpu.SemaphoreType.REGULAR, pltpu.SemaphoreType.REGULAR,
        ],
        compiler_params=pltpu.CompilerParams(
            collective_id=0, has_side_effects=True, vmem_limit_bytes=40 * 2**20),
    )(*given)
    grads = [pltpu.with_memory_space_constraint(item, pltpu.VMEM) for item in out]
    grads = pl.pallas_call(
        finish,
        out_shape=[jax.ShapeDtypeStruct(item.shape, item.dtype) for item in out],
        in_specs=[any_space] * 4,
        out_specs=[any_space] * 4,
        scratch_shapes=[dma((4,))],
        compiler_params=pltpu.CompilerParams(vmem_limit_bytes=2**20),
    )(*grads)
    return tuple(item.reshape(query.shape) for item in grads[:3]) + (grads[3],)


def solution(mesh):
    placed = P(None, "tm", "patch", None)
    return jax.shard_map(
        functools.partial(per_device, mesh.shape["patch"]),
        mesh=mesh,
        in_specs=(placed, placed, placed, placed, P()),
        out_specs=(placed, placed, placed, P()),
        check_vma=False,
    )
```

```python
import functools
import math

import jax
import jax.numpy as jnp
from jax import lax
from jax.experimental import pallas as pl
from jax.experimental.pallas import tpu as pltpu
from jax.sharding import PartitionSpec as P

MESH = pl.DeviceIdType.MESH
GROUP = 16
NEG = -1e30
FIRST, SHARER = 0, 1


def body(frames, span, parts, early, middle, q_hbm, k_hbm, v_hbm, g_hbm, bias_hbm, out, ob_ref,
         bias_ref, stage, held, back, table, acc, lows, mine, plane, total, shares,
         load_sem, in_sem, in_sent, out_sem, out_sent, plane_sem, plane_sent, share_sem, share_sent,
         bias_sem, go_sem, world_sem):
    me = lax.axis_index("tm")
    place = lax.axis_index("patch")
    rows, dim = held.shape[2], held.shape[3]
    inputs = (q_hbm, k_hbm, v_hbm, g_hbm)
    scale = 1.0 / math.sqrt(dim)

    def rows_of(block):
        return pl.ds(pl.multiple_of(block * GROUP, GROUP), GROUP)

    def head_columns(head):
        return pl.ds(pl.multiple_of(head * dim, dim), dim)

    bias_copy = pltpu.make_async_copy(bias_hbm, bias_ref, bias_sem)
    bias_copy.start()
    loads = [pltpu.make_async_copy(ref, stage.at[a], load_sem.at[a]) for a, ref in enumerate(inputs)]
    for load in loads:
        load.start()

    barrier = pltpu.get_barrier_semaphore()
    for off in range(1, frames):
        peer = lax.rem(me + off, frames)

        @pl.when(peer != SHARER)
        def _():
            pl.semaphore_signal(barrier, inc=1, device_id={"tm": peer}, device_id_type=MESH)

    @pl.when(me != SHARER)
    def _():
        pl.semaphore_wait(barrier, frames - 1)

    @pl.when(me == FIRST)
    def _():
        pl.semaphore_signal(go_sem, inc=1, device_id={"tm": SHARER}, device_id_type=MESH)

    @pl.when(me == SHARER)
    def _():
        pl.semaphore_wait(go_sem, 1)
        for off in range(1, span):
            pl.semaphore_signal(barrier, inc=1, device_id={"patch": lax.rem(place + off, span)}, device_id_type=MESH)

    for load in loads:
        load.wait()

    def send_part(part, carry):
        part_rows = rows_of(part)
        pltpu.make_async_copy(
            stage.at[:, part_rows, head_columns(me)], held.at[:, me, part_rows], in_sem.at[part]).start()
        for off in range(1, frames):
            head = lax.rem(me + off, frames)
            pltpu.make_async_remote_copy(
                src_ref=stage.at[:, part_rows, head_columns(head)],
                dst_ref=held.at[:, me, part_rows],
                send_sem=in_sent, recv_sem=in_sem.at[part],
                device_id={"tm": head}, device_id_type=MESH).start()
        return carry

    lax.fori_loop(0, parts, send_part, 0)

    size = frames * GROUP
    u_row = lax.broadcasted_iota(jnp.int32, (size, size), 0)
    t_col = lax.broadcasted_iota(jnp.int32, (size, size), 1)
    same = (u_row % GROUP) == (t_col % GROUP)
    offset = jnp.where(same, t_col // GROUP - u_row // GROUP, -1)
    bias_copy.wait()
    filled = jnp.full((size, size), NEG, jnp.float32)
    for d in range(frames):
        filled = jnp.where(offset == d, bias_ref[me, d], filled)
    table[...] = filled
    acc[...] = jnp.zeros_like(acc)

    contract_last = (((1,), (1,)), ((), ()))
    contract_first = (((0,), (0,)), ((), ()))

    def block_of(a, block):
        return held[a, :, rows_of(block), :].reshape(size, dim)

    def weigh(block):
        q, k, v, g = (block_of(a, block) for a in range(4))
        scores = lax.dot_general(k, q, contract_last, preferred_element_type=jnp.float32) * scale + table[...]
        expon = jnp.exp(scores - jnp.max(scores, axis=0, keepdims=True))
        weights = expon * (1.0 / jnp.sum(expon, axis=0, keepdims=True))
        low = weights.astype(jnp.bfloat16)
        grad_weights = lax.dot_general(v, g, contract_last, preferred_element_type=jnp.float32)
        rowdot = jnp.sum(low.astype(jnp.float32) * grad_weights, axis=0, keepdims=True)
        grad_scores = weights * (grad_weights - rowdot)
        acc[...] += grad_scores
        return low, grad_scores.astype(jnp.bfloat16)

    def gradients(block, low, grad_low):
        q, k, g = (block_of(a, block) for a in (0, 1, 3))
        dv = jnp.dot(low, g, preferred_element_type=jnp.float32)
        dk = jnp.dot(grad_low, q, preferred_element_type=jnp.float32) * scale
        dq = lax.dot_general(grad_low, k, contract_first, preferred_element_type=jnp.float32) * scale
        for a, grad in enumerate((dq, dk, dv)):
            back[a, :, rows_of(block), :] = grad.astype(jnp.bfloat16).reshape(frames, GROUP, dim)

    def send_back(part, carry):
        part_rows = rows_of(part)
        for off in range(1, frames):
            frame = lax.rem(me + off, frames)
            pltpu.make_async_remote_copy(
                src_ref=back.at[:, frame, part_rows],
                dst_ref=out.at[:, part_rows, head_columns(me)],
                send_sem=out_sent, recv_sem=out_sem,
                device_id={"tm": frame}, device_id_type=MESH).start()
        pltpu.make_async_copy(back.at[:, me, part_rows], out.at[:, part_rows, head_columns(me)], out_sem).start()
        return carry

    def await_part(part):
        here = held.at[:, :, rows_of(part)]
        pltpu.make_async_copy(here, here, in_sem.at[part]).wait()

    def work_part(part, carry):
        await_part(part)
        gradients(part, *weigh(part))

        @pl.when(jnp.logical_and(part == parts - 2, me == SHARER))
        def _():
            pl.semaphore_wait(barrier, span - 1)
            for off in range(1, frames):
                pl.semaphore_signal(
                    world_sem, inc=1, device_id={"tm": lax.rem(me + off, frames)}, device_id_type=MESH)

        return carry

    last = parts - 1
    lax.fori_loop(0, last, work_part, 0)
    lax.fori_loop(0, early, send_back, 0)
    await_part(last)
    low, grad_low = weigh(last)
    lows[0] = low
    lows[1] = grad_low

    by_frame = jnp.sum(acc[...].reshape(frames, GROUP, size), axis=1)
    u_small = lax.broadcasted_iota(jnp.int32, (frames, size), 0)
    t_small = lax.broadcasted_iota(jnp.int32, (frames, size), 1) // GROUP
    sums = [jnp.sum(jnp.where(t_small - u_small == d, by_frame, 0.0), axis=0, keepdims=True) for d in range(frames)]
    width = frames * frames
    spread = jnp.concatenate(sums * frames, axis=0)
    row = lax.dot_general(
        jnp.ones((8, size), jnp.float32), spread, contract_last,
        precision=lax.Precision.HIGHEST, preferred_element_type=jnp.float32)[0:1]
    lane = lax.broadcasted_iota(jnp.int32, (1, width), 1)
    mine[...] = jnp.where(lane // frames == me, row, 0.0)

    pltpu.make_async_copy(mine, plane.at[me], plane_sem).start()
    for off in range(1, frames):
        pltpu.make_async_remote_copy(
            src_ref=mine, dst_ref=plane.at[me], send_sem=plane_sent, recv_sem=plane_sem,
            device_id={"tm": lax.rem(me + off, frames)}, device_id_type=MESH).start()
    gradients(last, lows[0], lows[1])
    lax.fori_loop(early, middle, send_back, 0)
    pltpu.make_async_copy(plane, plane, plane_sem).wait()
    total[...] = jnp.sum(plane[...], axis=0)

    @pl.when(me != SHARER)
    def _():
        pl.semaphore_wait(world_sem, 1)

    pltpu.make_async_copy(total, shares.at[place], share_sem).start()
    for off in sorted(range(1, span), key=lambda off: -min(off, span - off)):
        pltpu.make_async_remote_copy(
            src_ref=total, dst_ref=shares.at[place], send_sem=share_sent, recv_sem=share_sem,
            device_id={"patch": lax.rem(place + off, span)}, device_id_type=MESH).start()
    lax.fori_loop(middle, parts, send_back, 0)
    pltpu.make_async_copy(shares, shares, share_sem).wait()
    table_sum = jnp.sum(shares[...], axis=0)
    for h in range(frames):
        ob_ref[pl.ds(h, 1), :] = table_sum[:, h * frames : (h + 1) * frames]
    sent = plane.at[pl.ds(0, frames - 1)]
    pltpu.make_async_copy(sent, sent, plane_sent).wait()
    sent = shares.at[pl.ds(0, span - 1)]
    pltpu.make_async_copy(sent, sent, share_sent).wait()

    sent = held.at[:, pl.ds(0, frames - 1)]
    pltpu.make_async_copy(sent, sent, in_sent).wait()
    sent = back.at[:, pl.ds(0, frames - 1)]
    pltpu.make_async_copy(sent, sent, out_sent).wait()
    pltpu.make_async_copy(out, out, out_sem).wait()


def finish(*refs):
    grads, bias, targets, sem = refs[0], refs[1], refs[2:6], refs[6]
    sources = [grads.at[a] for a in range(3)] + [bias]
    copies = [pltpu.make_async_copy(a, b, sem.at[i]) for i, (a, b) in enumerate(zip(sources, targets))]
    for copy in copies:
        copy.start()
    for copy in copies:
        copy.wait()


def per_device(span, query, key, value, grad, time_bias):
    clips, _, patches, width = query.shape
    heads, frames = time_bias.shape
    dim = width // heads
    rows = clips * patches
    given = [item.reshape(rows, width) for item in (query, key, value, grad)] + [time_bias]
    given = [pltpu.with_memory_space_constraint(item, pltpu.HBM) for item in given]
    parts, early, middle = rows // GROUP, 1, 3
    any_space = pl.BlockSpec(memory_space=pl.ANY)
    size = frames * GROUP
    dma = pltpu.SemaphoreType.DMA
    out = pl.pallas_call(
        functools.partial(body, frames, span, parts, early, middle),
        out_shape=[
            jax.ShapeDtypeStruct((3, rows, width), jnp.bfloat16), jax.ShapeDtypeStruct((heads, frames), jnp.float32)],
        in_specs=[any_space] * 5,
        out_specs=[any_space] + [pl.BlockSpec(memory_space=pltpu.VMEM)],
        scratch_shapes=[
            pltpu.SMEM((heads, frames), jnp.float32),
            pltpu.VMEM((4, rows, width), jnp.bfloat16),
            pltpu.VMEM((4, frames, rows, dim), jnp.bfloat16),
            pltpu.VMEM((3, frames, rows, dim), jnp.bfloat16),
            pltpu.VMEM((size, size), jnp.float32),
            pltpu.VMEM((size, size), jnp.float32),
            pltpu.VMEM((2, size, size), jnp.bfloat16),
            pltpu.VMEM((1, heads * frames), jnp.float32),
            pltpu.VMEM((frames, 1, heads * frames), jnp.float32),
            pltpu.VMEM((1, heads * frames), jnp.float32),
            pltpu.VMEM((span, 1, heads * frames), jnp.float32),
            dma((4,)), dma((parts,)), dma, dma, dma, dma, dma, dma, dma, dma,
            pltpu.SemaphoreType.REGULAR, pltpu.SemaphoreType.REGULAR,
        ],
        compiler_params=pltpu.CompilerParams(
            collective_id=0, has_side_effects=True, vmem_limit_bytes=40 * 2**20),
    )(*given)
    grads = [pltpu.with_memory_space_constraint(item, pltpu.VMEM) for item in out]
    grads = pl.pallas_call(
        finish,
        out_shape=[jax.ShapeDtypeStruct((rows, width), jnp.bfloat16)] * 3
        + [jax.ShapeDtypeStruct((heads, frames), jnp.float32)],
        in_specs=[any_space] * 2,
        out_specs=[any_space] * 4,
        scratch_shapes=[dma((4,))],
        compiler_params=pltpu.CompilerParams(vmem_limit_bytes=2**20),
    )(*grads)
    return tuple(item.reshape(query.shape) for item in grads[:3]) + (grads[3],)


def solution(mesh):
    placed = P(None, "tm", "patch", None)
    return jax.shard_map(
        functools.partial(per_device, mesh.shape["patch"]),
        mesh=mesh,
        in_specs=(placed, placed, placed, placed, P()),
        out_specs=(placed, placed, placed, P()),
        check_vma=False,
    )
```

```python
import functools
import math

import jax
import jax.numpy as jnp
from jax import lax
from jax.experimental import pallas as pl
from jax.experimental.pallas import tpu as pltpu
from jax.sharding import PartitionSpec as P

MESH = pl.DeviceIdType.MESH
GROUP = 16
NEG = -1e30
FIRST, SHARER = 0, 1


def body(frames, span, parts, early, middle, q_hbm, k_hbm, v_hbm, g_hbm, bias_hbm, out, ob_ref,
         bias_ref, stage, held, back, table, acc, lows, mine, plane, total, shares,
         load_sem, in_sem, in_sent, out_sem, out_sent, plane_sem, plane_sent, share_sem, share_sent,
         bias_sem, go_sem, world_sem):
    me = lax.axis_index("tm")
    place = lax.axis_index("patch")
    rows, dim = held.shape[2], held.shape[3]
    inputs = (q_hbm, k_hbm, v_hbm, g_hbm)
    scale = 1.0 / math.sqrt(dim)

    def rows_of(block):
        return pl.ds(pl.multiple_of(block * GROUP, GROUP), GROUP)

    def head_columns(head):
        return pl.ds(pl.multiple_of(head * dim, dim), dim)

    bias_copy = pltpu.make_async_copy(bias_hbm, bias_ref, bias_sem)
    bias_copy.start()
    loads = [pltpu.make_async_copy(ref, stage.at[a], load_sem.at[a]) for a, ref in enumerate(inputs)]
    for load in loads:
        load.start()

    barrier = pltpu.get_barrier_semaphore()
    for off in range(1, frames):
        peer = lax.rem(me + off, frames)

        @pl.when(peer != SHARER)
        def _():
            pl.semaphore_signal(barrier, inc=1, device_id={"tm": peer}, device_id_type=MESH)

    @pl.when(me != SHARER)
    def _():
        pl.semaphore_wait(barrier, frames - 1)

    @pl.when(me == FIRST)
    def _():
        pl.semaphore_signal(go_sem, inc=1, device_id={"tm": SHARER}, device_id_type=MESH)

    @pl.when(me == SHARER)
    def _():
        pl.semaphore_wait(go_sem, 1)
        for off in range(1, span):
            pl.semaphore_signal(barrier, inc=1, device_id={"patch": lax.rem(place + off, span)}, device_id_type=MESH)

    for load in loads:
        load.wait()

    def send_part(part, carry):
        part_rows = rows_of(part)
        pltpu.make_async_copy(
            stage.at[:, part_rows, head_columns(me)], held.at[:, me, part_rows], in_sem.at[part]).start()
        for off in range(1, frames):
            head = lax.rem(me + off, frames)
            pltpu.make_async_remote_copy(
                src_ref=stage.at[:, part_rows, head_columns(head)],
                dst_ref=held.at[:, me, part_rows],
                send_sem=in_sent, recv_sem=in_sem.at[part],
                device_id={"tm": head}, device_id_type=MESH).start()
        return carry

    lax.fori_loop(0, parts, send_part, 0)

    size = frames * GROUP
    u_row = lax.broadcasted_iota(jnp.int32, (size, size), 0)
    t_col = lax.broadcasted_iota(jnp.int32, (size, size), 1)
    same = (u_row % GROUP) == (t_col % GROUP)
    offset = jnp.where(same, t_col // GROUP - u_row // GROUP, -1)
    bias_copy.wait()
    filled = jnp.full((size, size), NEG, jnp.float32)
    for d in range(frames):
        filled = jnp.where(offset == d, bias_ref[me, d], filled)
    table[...] = filled
    acc[...] = jnp.zeros_like(acc)

    contract_last = (((1,), (1,)), ((), ()))
    contract_first = (((0,), (0,)), ((), ()))

    def block_of(a, block):
        return held[a, :, rows_of(block), :].reshape(size, dim)

    def weigh(block):
        q, k, v, g = (block_of(a, block) for a in range(4))
        scores = lax.dot_general(k, q, contract_last, preferred_element_type=jnp.float32) * scale + table[...]
        expon = jnp.exp(scores - jnp.max(scores, axis=0, keepdims=True))
        weights = expon * (1.0 / jnp.sum(expon, axis=0, keepdims=True))
        low = weights.astype(jnp.bfloat16)
        grad_weights = lax.dot_general(v, g, contract_last, preferred_element_type=jnp.float32)
        rowdot = jnp.sum(low.astype(jnp.float32) * grad_weights, axis=0, keepdims=True)
        grad_scores = weights * (grad_weights - rowdot)
        acc[...] += grad_scores
        return low, grad_scores.astype(jnp.bfloat16)

    def gradients(block, low, grad_low):
        q, k, g = (block_of(a, block) for a in (0, 1, 3))
        dv = jnp.dot(low, g, preferred_element_type=jnp.float32)
        dk = jnp.dot(grad_low, q, preferred_element_type=jnp.float32) * scale
        dq = lax.dot_general(grad_low, k, contract_first, preferred_element_type=jnp.float32) * scale
        for a, grad in enumerate((dq, dk, dv)):
            back[a, :, rows_of(block), :] = grad.astype(jnp.bfloat16).reshape(frames, GROUP, dim)

    def send_back(part, carry):
        part_rows = rows_of(part)
        for off in range(1, frames):
            frame = lax.rem(me + off, frames)
            pltpu.make_async_remote_copy(
                src_ref=back.at[:, frame, part_rows],
                dst_ref=out.at[:, part_rows, head_columns(me)],
                send_sem=out_sent, recv_sem=out_sem,
                device_id={"tm": frame}, device_id_type=MESH).start()
        pltpu.make_async_copy(back.at[:, me, part_rows], out.at[:, part_rows, head_columns(me)], out_sem).start()
        return carry

    def await_part(part):
        here = held.at[:, :, rows_of(part)]
        pltpu.make_async_copy(here, here, in_sem.at[part]).wait()

    def work_part(part, carry):
        await_part(part)
        gradients(part, *weigh(part))

        @pl.when(jnp.logical_and(part == parts - 2, me == SHARER))
        def _():
            pl.semaphore_wait(barrier, span - 1)
            for off in range(1, frames):
                pl.semaphore_signal(
                    world_sem, inc=1, device_id={"tm": lax.rem(me + off, frames)}, device_id_type=MESH)

        return carry

    last = parts - 1
    lax.fori_loop(0, last, work_part, 0)
    lax.fori_loop(0, early, send_back, 0)
    await_part(last)
    low, grad_low = weigh(last)
    lows[0] = low
    lows[1] = grad_low

    by_frame = jnp.sum(acc[...].reshape(frames, GROUP, size), axis=1)
    u_small = lax.broadcasted_iota(jnp.int32, (frames, size), 0)
    t_small = lax.broadcasted_iota(jnp.int32, (frames, size), 1) // GROUP
    sums = [jnp.sum(jnp.where(t_small - u_small == d, by_frame, 0.0), axis=0, keepdims=True) for d in range(frames)]
    width = frames * frames
    spread = jnp.concatenate(sums * frames, axis=0)
    row = lax.dot_general(
        jnp.ones((8, size), jnp.float32), spread, contract_last,
        precision=lax.Precision.HIGHEST, preferred_element_type=jnp.float32)[0:1]
    lane = lax.broadcasted_iota(jnp.int32, (1, width), 1)
    mine[...] = jnp.where(lane // frames == me, row, 0.0)

    @pl.when(me != SHARER)
    def _():
        pl.semaphore_wait(world_sem, 1)

    side, z = lax.rem(place, 2), place // 2
    pltpu.make_async_copy(mine, plane.at[side * frames + me], plane_sem).start()
    for other, off in [(1, off) for off in range(frames)] + [(0, off) for off in range(1, frames)]:
        target = {"tm": lax.rem(me + off, frames), "patch": 2 * z + lax.rem(side + other, 2)}
        pltpu.make_async_remote_copy(
            src_ref=mine, dst_ref=plane.at[side * frames + me], send_sem=plane_sent, recv_sem=plane_sem,
            device_id=target, device_id_type=MESH).start()
    gradients(last, lows[0], lows[1])
    lax.fori_loop(early, middle, send_back, 0)
    pltpu.make_async_copy(plane, plane, plane_sem).wait()
    total[...] = jnp.sum(plane[...], axis=0)
    pltpu.make_async_copy(total, shares.at[z], share_sem).start()
    for off in sorted(range(1, span // 2), key=lambda off: -min(off, span // 2 - off)):
        pltpu.make_async_remote_copy(
            src_ref=total, dst_ref=shares.at[z], send_sem=share_sent, recv_sem=share_sem,
            device_id={"patch": 2 * lax.rem(z + off, span // 2) + side}, device_id_type=MESH).start()
    lax.fori_loop(middle, parts, send_back, 0)
    pltpu.make_async_copy(shares, shares, share_sem).wait()
    table_sum = jnp.sum(shares[...], axis=0)
    for h in range(frames):
        ob_ref[pl.ds(h, 1), :] = table_sum[:, h * frames : (h + 1) * frames]
    sent = plane.at[pl.ds(0, 2 * frames - 1)]
    pltpu.make_async_copy(sent, sent, plane_sent).wait()
    sent = shares.at[pl.ds(0, span // 2 - 1)]
    pltpu.make_async_copy(sent, sent, share_sent).wait()

    sent = held.at[:, pl.ds(0, frames - 1)]
    pltpu.make_async_copy(sent, sent, in_sent).wait()
    sent = back.at[:, pl.ds(0, frames - 1)]
    pltpu.make_async_copy(sent, sent, out_sent).wait()
    pltpu.make_async_copy(out, out, out_sem).wait()


def finish(*refs):
    grads, bias, targets, sem = refs[0], refs[1], refs[2:6], refs[6]
    sources = [grads.at[a] for a in range(3)] + [bias]
    copies = [pltpu.make_async_copy(a, b, sem.at[i]) for i, (a, b) in enumerate(zip(sources, targets))]
    for copy in copies:
        copy.start()
    for copy in copies:
        copy.wait()


def per_device(span, query, key, value, grad, time_bias):
    clips, _, patches, width = query.shape
    heads, frames = time_bias.shape
    dim = width // heads
    rows = clips * patches
    given = [item.reshape(rows, width) for item in (query, key, value, grad)] + [time_bias]
    given = [pltpu.with_memory_space_constraint(item, pltpu.HBM) for item in given]
    parts, early, middle = rows // GROUP, 1, 3
    any_space = pl.BlockSpec(memory_space=pl.ANY)
    size = frames * GROUP
    dma = pltpu.SemaphoreType.DMA
    out = pl.pallas_call(
        functools.partial(body, frames, span, parts, early, middle),
        out_shape=[
            jax.ShapeDtypeStruct((3, rows, width), jnp.bfloat16), jax.ShapeDtypeStruct((heads, frames), jnp.float32)],
        in_specs=[any_space] * 5,
        out_specs=[any_space] + [pl.BlockSpec(memory_space=pltpu.VMEM)],
        scratch_shapes=[
            pltpu.SMEM((heads, frames), jnp.float32),
            pltpu.VMEM((4, rows, width), jnp.bfloat16),
            pltpu.VMEM((4, frames, rows, dim), jnp.bfloat16),
            pltpu.VMEM((3, frames, rows, dim), jnp.bfloat16),
            pltpu.VMEM((size, size), jnp.float32),
            pltpu.VMEM((size, size), jnp.float32),
            pltpu.VMEM((2, size, size), jnp.bfloat16),
            pltpu.VMEM((1, heads * frames), jnp.float32),
            pltpu.VMEM((2 * frames, 1, heads * frames), jnp.float32),
            pltpu.VMEM((1, heads * frames), jnp.float32),
            pltpu.VMEM((span // 2, 1, heads * frames), jnp.float32),
            dma((4,)), dma((parts,)), dma, dma, dma, dma, dma, dma, dma, dma,
            pltpu.SemaphoreType.REGULAR, pltpu.SemaphoreType.REGULAR,
        ],
        compiler_params=pltpu.CompilerParams(
            collective_id=0, has_side_effects=True, vmem_limit_bytes=40 * 2**20),
    )(*given)
    grads = [pltpu.with_memory_space_constraint(item, pltpu.VMEM) for item in out]
    grads = pl.pallas_call(
        finish,
        out_shape=[jax.ShapeDtypeStruct((rows, width), jnp.bfloat16)] * 3
        + [jax.ShapeDtypeStruct((heads, frames), jnp.float32)],
        in_specs=[any_space] * 2,
        out_specs=[any_space] * 4,
        scratch_shapes=[dma((4,))],
        compiler_params=pltpu.CompilerParams(vmem_limit_bytes=2**20),
    )(*grads)
    return tuple(item.reshape(query.shape) for item in grads[:3]) + (grads[3],)


def solution(mesh):
    placed = P(None, "tm", "patch", None)
    return jax.shard_map(
        functools.partial(per_device, mesh.shape["patch"]),
        mesh=mesh,
        in_specs=(placed, placed, placed, placed, P()),
        out_specs=(placed, placed, placed, P()),
        check_vma=False,
    )
```

```python
import functools
import math

import jax
import jax.numpy as jnp
from jax import lax
from jax.experimental import pallas as pl
from jax.experimental.pallas import tpu as pltpu
from jax.sharding import PartitionSpec as P

MESH = pl.DeviceIdType.MESH
GROUP = 16
NEG = -1e30
FIRST, SHARER = 0, 1


def body(frames, span, parts, early, middle, q_hbm, k_hbm, v_hbm, g_hbm, bias_hbm, out, ob_ref,
         bias_ref, stage, held, back, table, acc, lows, mine, plane, total, shares,
         load_sem, in_sem, in_sent, out_sem, out_sent, plane_sem, plane_sent, share_sem, share_sent,
         bias_sem, go_sem, world_sem):
    me = lax.axis_index("tm")
    place = lax.axis_index("patch")
    rows, dim = held.shape[2], held.shape[3]
    inputs = (q_hbm, k_hbm, v_hbm, g_hbm)
    scale = 1.0 / math.sqrt(dim)

    def rows_of(block):
        return pl.ds(pl.multiple_of(block * GROUP, GROUP), GROUP)

    def head_columns(head):
        return pl.ds(pl.multiple_of(head * dim, dim), dim)

    bias_copy = pltpu.make_async_copy(bias_hbm, bias_ref, bias_sem)
    bias_copy.start()
    first_rows, other_rows = pl.ds(0, GROUP), pl.ds(GROUP, rows - GROUP)
    for i, some in enumerate((first_rows, other_rows)):
        for a, ref in enumerate(inputs):
            pltpu.make_async_copy(ref.at[some], stage.at[a, some], load_sem.at[i]).start()

    barrier = pltpu.get_barrier_semaphore()
    for off in range(1, frames):
        peer = lax.rem(me + off, frames)

        @pl.when(peer != SHARER)
        def _():
            pl.semaphore_signal(barrier, inc=1, device_id={"tm": peer}, device_id_type=MESH)

    @pl.when(me != SHARER)
    def _():
        pl.semaphore_wait(barrier, frames - 1)

    @pl.when(me == FIRST)
    def _():
        pl.semaphore_signal(go_sem, inc=1, device_id={"tm": SHARER}, device_id_type=MESH)

    @pl.when(me == SHARER)
    def _():
        pl.semaphore_wait(go_sem, 1)
        for off in range(1, span):
            pl.semaphore_signal(barrier, inc=1, device_id={"patch": lax.rem(place + off, span)}, device_id_type=MESH)

    def send_part(part, carry):
        part_rows = rows_of(part)
        pltpu.make_async_copy(
            stage.at[:, part_rows, head_columns(me)], held.at[:, me, part_rows], in_sem.at[part]).start()
        for off in range(1, frames):
            head = lax.rem(me + off, frames)
            pltpu.make_async_remote_copy(
                src_ref=stage.at[:, part_rows, head_columns(head)],
                dst_ref=held.at[:, me, part_rows],
                send_sem=in_sent, recv_sem=in_sem.at[part],
                device_id={"tm": head}, device_id_type=MESH).start()
        return carry

    here = stage.at[:, first_rows]
    pltpu.make_async_copy(here, here, load_sem.at[0]).wait()
    send_part(0, 0)
    here = stage.at[:, other_rows]
    pltpu.make_async_copy(here, here, load_sem.at[1]).wait()
    lax.fori_loop(1, parts, send_part, 0)

    size = frames * GROUP
    u_row = lax.broadcasted_iota(jnp.int32, (size, size), 0)
    t_col = lax.broadcasted_iota(jnp.int32, (size, size), 1)
    same = (u_row % GROUP) == (t_col % GROUP)
    offset = jnp.where(same, t_col // GROUP - u_row // GROUP, -1)
    bias_copy.wait()
    filled = jnp.full((size, size), NEG, jnp.float32)
    for d in range(frames):
        filled = jnp.where(offset == d, bias_ref[me, d], filled)
    table[...] = filled
    acc[...] = jnp.zeros_like(acc)

    contract_last = (((1,), (1,)), ((), ()))
    contract_first = (((0,), (0,)), ((), ()))

    def block_of(a, block):
        return held[a, :, rows_of(block), :].reshape(size, dim)

    def weigh(block):
        q, k, v, g = (block_of(a, block) for a in range(4))
        scores = lax.dot_general(k, q, contract_last, preferred_element_type=jnp.float32) * scale + table[...]
        expon = jnp.exp(scores - jnp.max(scores, axis=0, keepdims=True))
        weights = expon * (1.0 / jnp.sum(expon, axis=0, keepdims=True))
        low = weights.astype(jnp.bfloat16)
        grad_weights = lax.dot_general(v, g, contract_last, preferred_element_type=jnp.float32)
        rowdot = jnp.sum(low.astype(jnp.float32) * grad_weights, axis=0, keepdims=True)
        grad_scores = weights * (grad_weights - rowdot)
        acc[...] += grad_scores
        return low, grad_scores.astype(jnp.bfloat16)

    def gradients(block, low, grad_low):
        q, k, g = (block_of(a, block) for a in (0, 1, 3))
        dv = jnp.dot(low, g, preferred_element_type=jnp.float32)
        dk = jnp.dot(grad_low, q, preferred_element_type=jnp.float32) * scale
        dq = lax.dot_general(grad_low, k, contract_first, preferred_element_type=jnp.float32) * scale
        for a, grad in enumerate((dq, dk, dv)):
            back[a, :, rows_of(block), :] = grad.astype(jnp.bfloat16).reshape(frames, GROUP, dim)

    def send_back(part, carry):
        part_rows = rows_of(part)
        for off in range(1, frames):
            frame = lax.rem(me + off, frames)
            pltpu.make_async_remote_copy(
                src_ref=back.at[:, frame, part_rows],
                dst_ref=out.at[:, part_rows, head_columns(me)],
                send_sem=out_sent, recv_sem=out_sem,
                device_id={"tm": frame}, device_id_type=MESH).start()
        pltpu.make_async_copy(back.at[:, me, part_rows], out.at[:, part_rows, head_columns(me)], out_sem).start()
        return carry

    def await_part(part):
        here = held.at[:, :, rows_of(part)]
        pltpu.make_async_copy(here, here, in_sem.at[part]).wait()

    def work_part(part, carry):
        await_part(part)
        gradients(part, *weigh(part))

        @pl.when(jnp.logical_and(part == parts - 2, me == SHARER))
        def _():
            pl.semaphore_wait(barrier, span - 1)
            for off in range(1, frames):
                pl.semaphore_signal(
                    world_sem, inc=1, device_id={"tm": lax.rem(me + off, frames)}, device_id_type=MESH)

        return carry

    last = parts - 1
    lax.fori_loop(0, last, work_part, 0)
    lax.fori_loop(0, early, send_back, 0)
    await_part(last)
    low, grad_low = weigh(last)
    lows[0] = low
    lows[1] = grad_low

    by_frame = jnp.sum(acc[...].reshape(frames, GROUP, size), axis=1)
    u_small = lax.broadcasted_iota(jnp.int32, (frames, size), 0)
    t_small = lax.broadcasted_iota(jnp.int32, (frames, size), 1) // GROUP
    sums = [jnp.sum(jnp.where(t_small - u_small == d, by_frame, 0.0), axis=0, keepdims=True) for d in range(frames)]
    width = frames * frames
    spread = jnp.concatenate(sums * frames, axis=0)
    row = lax.dot_general(
        jnp.ones((8, size), jnp.float32), spread, contract_last,
        precision=lax.Precision.HIGHEST, preferred_element_type=jnp.float32)[0:1]
    lane = lax.broadcasted_iota(jnp.int32, (1, width), 1)
    mine[...] = jnp.where(lane // frames == me, row, 0.0)

    @pl.when(me != SHARER)
    def _():
        pl.semaphore_wait(world_sem, 1)

    side, z = lax.rem(place, 2), place // 2
    pltpu.make_async_copy(mine, plane.at[side * frames + me], plane_sem).start()
    for other, off in [(1, off) for off in range(frames)] + [(0, off) for off in range(1, frames)]:
        target = {"tm": lax.rem(me + off, frames), "patch": 2 * z + lax.rem(side + other, 2)}
        pltpu.make_async_remote_copy(
            src_ref=mine, dst_ref=plane.at[side * frames + me], send_sem=plane_sent, recv_sem=plane_sem,
            device_id=target, device_id_type=MESH).start()
    gradients(last, lows[0], lows[1])
    lax.fori_loop(early, middle, send_back, 0)
    pltpu.make_async_copy(plane, plane, plane_sem).wait()
    total[...] = jnp.sum(plane[...], axis=0)
    pltpu.make_async_copy(total, shares.at[z], share_sem).start()
    for off in sorted(range(1, span // 2), key=lambda off: -min(off, span // 2 - off)):
        pltpu.make_async_remote_copy(
            src_ref=total, dst_ref=shares.at[z], send_sem=share_sent, recv_sem=share_sem,
            device_id={"patch": 2 * lax.rem(z + off, span // 2) + side}, device_id_type=MESH).start()
    lax.fori_loop(middle, parts, send_back, 0)
    pltpu.make_async_copy(shares, shares, share_sem).wait()
    table_sum = jnp.sum(shares[...], axis=0)
    for h in range(frames):
        ob_ref[pl.ds(h, 1), :] = table_sum[:, h * frames : (h + 1) * frames]
    sent = plane.at[pl.ds(0, 2 * frames - 1)]
    pltpu.make_async_copy(sent, sent, plane_sent).wait()
    sent = shares.at[pl.ds(0, span // 2 - 1)]
    pltpu.make_async_copy(sent, sent, share_sent).wait()

    sent = held.at[:, pl.ds(0, frames - 1)]
    pltpu.make_async_copy(sent, sent, in_sent).wait()
    sent = back.at[:, pl.ds(0, frames - 1)]
    pltpu.make_async_copy(sent, sent, out_sent).wait()
    pltpu.make_async_copy(out, out, out_sem).wait()


def finish(*refs):
    grads, bias, targets, sem = refs[0], refs[1], refs[2:6], refs[6]
    sources = [grads.at[a] for a in range(3)] + [bias]
    copies = [pltpu.make_async_copy(a, b, sem.at[i]) for i, (a, b) in enumerate(zip(sources, targets))]
    for copy in copies:
        copy.start()
    for copy in copies:
        copy.wait()


def per_device(span, query, key, value, grad, time_bias):
    clips, _, patches, width = query.shape
    heads, frames = time_bias.shape
    dim = width // heads
    rows = clips * patches
    given = [item.reshape(rows, width) for item in (query, key, value, grad)] + [time_bias]
    given = [pltpu.with_memory_space_constraint(item, pltpu.HBM) for item in given]
    parts, early, middle = rows // GROUP, 1, 3
    any_space = pl.BlockSpec(memory_space=pl.ANY)
    size = frames * GROUP
    dma = pltpu.SemaphoreType.DMA
    out = pl.pallas_call(
        functools.partial(body, frames, span, parts, early, middle),
        out_shape=[
            jax.ShapeDtypeStruct((3, rows, width), jnp.bfloat16), jax.ShapeDtypeStruct((heads, frames), jnp.float32)],
        in_specs=[any_space] * 5,
        out_specs=[any_space] + [pl.BlockSpec(memory_space=pltpu.VMEM)],
        scratch_shapes=[
            pltpu.SMEM((heads, frames), jnp.float32),
            pltpu.VMEM((4, rows, width), jnp.bfloat16),
            pltpu.VMEM((4, frames, rows, dim), jnp.bfloat16),
            pltpu.VMEM((3, frames, rows, dim), jnp.bfloat16),
            pltpu.VMEM((size, size), jnp.float32),
            pltpu.VMEM((size, size), jnp.float32),
            pltpu.VMEM((2, size, size), jnp.bfloat16),
            pltpu.VMEM((1, heads * frames), jnp.float32),
            pltpu.VMEM((2 * frames, 1, heads * frames), jnp.float32),
            pltpu.VMEM((1, heads * frames), jnp.float32),
            pltpu.VMEM((span // 2, 1, heads * frames), jnp.float32),
            dma((2,)), dma((parts,)), dma, dma, dma, dma, dma, dma, dma, dma,
            pltpu.SemaphoreType.REGULAR, pltpu.SemaphoreType.REGULAR,
        ],
        compiler_params=pltpu.CompilerParams(
            collective_id=0, has_side_effects=True, vmem_limit_bytes=40 * 2**20),
    )(*given)
    grads = [pltpu.with_memory_space_constraint(item, pltpu.VMEM) for item in out]
    grads = pl.pallas_call(
        finish,
        out_shape=[jax.ShapeDtypeStruct((rows, width), jnp.bfloat16)] * 3
        + [jax.ShapeDtypeStruct((heads, frames), jnp.float32)],
        in_specs=[any_space] * 2,
        out_specs=[any_space] * 4,
        scratch_shapes=[dma((4,))],
        compiler_params=pltpu.CompilerParams(vmem_limit_bytes=2**20),
    )(*grads)
    return tuple(item.reshape(query.shape) for item in grads[:3]) + (grads[3],)


def solution(mesh):
    placed = P(None, "tm", "patch", None)
    return jax.shard_map(
        functools.partial(per_device, mesh.shape["patch"]),
        mesh=mesh,
        in_specs=(placed, placed, placed, placed, P()),
        out_specs=(placed, placed, placed, P()),
        check_vma=False,
    )
```
